512 devices in a mesh: cp: 128 (over y, z, core), hp: 4 (over x).
Axes of the slice: x: 4, y: 8, z: 8, core: 2. Of those that a mesh axis runs over, the one named last changes fastest.
Arguments:
- queries: bfloat16 [32768, 3072], P('cp', 'hp'), may hold values from -40 to 40
- key_rows: bfloat16 [32768, 3072], P('cp', 'hp'), may hold values from -4 to 4
- value_rows: bfloat16 [32768, 3072], P('cp', 'hp'), may hold values from -6 to 6
- out_grad: bfloat16 [32768, 3072], P('cp', 'hp'), may hold values from -6 to 6
- slot_stretch: int32 [256], replicated, may hold values from 0 to 255, as said below
- doc_id: int32 [256], replicated, may hold values from 0 to 255, as said below
- diag_kind: int32 [256], replicated, may hold values 0 or 1
Outputs:
- attended: bfloat16 [32768, 3072], P(('cp', 'hp'))
- query_grad: bfloat16 [32768, 3072], P(('cp', 'hp'))
- key_grad: bfloat16 [32768, 3072], P(('cp', 'hp'))
- value_grad: bfloat16 [32768, 3072], P(('cp', 'hp'))
The draws below stay inside these ranges and needn't reach their ends.
Inputs may be any that keep to these rules, and one draw needn't show every extreme that they name: `slot_stretch`: each stretch number once; the slots w * 16 to w * 16 + 15 hold the stretches w * 16 to w * 16 + 15 in some order. `doc_id`: a document's id is the number of its first stretch; it never falls from one stretch to the next and changes at every stretch w * 16, so no document spans two windows.
All inputs are finite; a program needn't handle non-finite values.
Results may differ from the reference program's by a relative error of at most 0.015.
The reference program's roundings to bfloat16 on the way (of `rounded`, `score_grad`, `key_term` and `value_term`) count: a program that leaves them out, or rounds other values in their place, can miss the bound.
Values may be sent and summed in bfloat16 or wider, within the bound.
A program may use at most 64 MiB of HBM per device.

```python
import math
import jax
import jax.numpy as jnp
from jax import lax

HEADS = 24
HEAD_DIM = 128
BLOCK = 128
WIN = 16
STRETCHES = 256
TOKENS = 32768


def shared_parts(key):
    features = HEADS * HEAD_DIM
    normal_base = jnp.clip(jax.random.normal(jax.random.fold_in(key, 11), (TOKENS, features), jnp.float32), -4.0, 4.0)
    return normal_base


def draw_key_rows(key, part):
    normal_base = shared_parts(key)
    return normal_base.astype(jnp.bfloat16)


def draw_queries(key, part):
    key = jax.random.fold_in(key, 5)
    return jnp.clip(jax.random.normal(key, (TOKENS, HEADS * HEAD_DIM), jnp.float32), -4.0, 4.0).astype(jnp.bfloat16)


def window_order(window_key):
    return jax.random.permutation(window_key, WIN)


def draw_slot_stretch(key, part):
    key = jax.random.fold_in(key, 7)
    windows = STRETCHES // WIN
    window_keys = jax.random.split(key, windows)
    orders = jax.vmap(window_order)(window_keys)
    offsets = (jnp.arange(windows) * WIN)[:, None]
    return (orders + offsets).reshape(STRETCHES).astype(jnp.int32)


def draw_doc_id(key, part):
    key = jax.random.fold_in(key, 9)
    stretch_index = jnp.arange(STRETCHES, dtype=jnp.int32)
    starts = jax.random.randint(key, (STRETCHES,), 0, 4) == 0
    starts = starts | (stretch_index % WIN == 0) | (stretch_index == STRETCHES - 1)
    first_stretch = jnp.where(starts, stretch_index, 0).astype(jnp.int32)
    return lax.cummax(first_stretch, axis=0).astype(jnp.int32)


def with_ends(entries, own_key, low, largest):
    longest = entries.shape.index(max(entries.shape))
    spots = []
    for shift in (0, 1):
        where = [jax.random.randint(jax.random.fold_in(own_key, axis), (), 0, length) for axis, length in enumerate(entries.shape)]
        where[longest] = (where[longest] + shift) % entries.shape[longest]
        spots.append(tuple(where))
    return entries.at[spots[0]].set(low).at[spots[1]].set(largest)


def block_levels(rng, shape, pieces, least, high):
    def one(position, shards_of):
        steps = jax.random.uniform(jax.random.fold_in(jax.random.fold_in(rng, 6), position), (shards_of,), jnp.float32, least / len(pieces), high / len(pieces))
        return jnp.repeat(jnp.exp(steps), shape[position] // shards_of).reshape((-1,) + (1,) * (len(shape) - position - 1))

    factor_of = one(*pieces[0])
    for cut in pieces[1:]:
        factor_of = factor_of * one(*cut)
    return factor_of


def centred(key, dims, spread, reach, pieces=(), held_as=jnp.bfloat16):
    entries = spread * jax.random.normal(key, dims, jnp.float32)
    if pieces:
        entries = entries * block_levels(key, dims, pieces, -0.22, 0.18)
    return jnp.clip(entries, -reach, reach).astype(held_as)


def setup_inputs(seed: int = 0) -> dict:
    splits = jax.random.split(jax.random.key(seed), 8)
    return {
        "queries": draw_queries(jax.random.fold_in(splits[7], 71), 0),
        "key_rows": draw_key_rows(jax.random.fold_in(splits[7], 71), 0),
        "value_rows": centred(splits[2], (TOKENS, HEADS * HEAD_DIM), 1.0, 6.0, ((0, 128), (1, 4))),
        "out_grad": centred(splits[3], (TOKENS, HEADS * HEAD_DIM), 1.0, 6.0, ((0, 128), (1, 4))),
        "slot_stretch": draw_slot_stretch(jax.random.fold_in(splits[7], 71), 0),
        "doc_id": draw_doc_id(jax.random.fold_in(splits[7], 71), 0),
        "diag_kind": with_ends((jax.random.randint(splits[6], (STRETCHES,), 0, 2) < 1).astype(jnp.int32), jax.random.fold_in(splits[6], 1), 0, 1),
    }


def head_pass(stacked, allowed):
    head_queries, head_keys, head_values, head_grads = stacked
    score_scale = 1.0 / math.sqrt(HEAD_DIM)
    window_rows = WIN * BLOCK
    wide_queries = head_queries.astype(jnp.float32)
    wide_keys = head_keys.astype(jnp.float32)
    wide_values = head_values.astype(jnp.float32)
    wide_grads = head_grads.astype(jnp.float32)
    scores = jnp.einsum('qd,kd->qk', wide_queries, wide_keys) * score_scale
    masked = jnp.where(allowed, scores, -1e+30)
    row_max = lax.optimization_barrier(jnp.max(masked, axis=1, keepdims=True))
    exponent = jnp.where(allowed, jnp.exp(masked - row_max), 0.0)
    weights = exponent / lax.optimization_barrier(jnp.sum(exponent, axis=1, keepdims=True))
    rounded = lax.optimization_barrier(weights.astype(jnp.bfloat16))
    attended = lax.optimization_barrier(jnp.einsum('qk,kd->qd', rounded.astype(jnp.float32), wide_values).astype(jnp.bfloat16))
    grad_dot = lax.optimization_barrier(jnp.sum(wide_grads * attended.astype(jnp.float32), axis=1, keepdims=True))
    weight_grad = jnp.einsum('qd,kd->qk', wide_grads, wide_values)
    score_grad = lax.optimization_barrier((weights * (weight_grad - grad_dot)).astype(jnp.bfloat16))
    wide_score_grad = score_grad.astype(jnp.float32)
    query_grad = (jnp.einsum('qk,kd->qd', wide_score_grad, wide_keys) * score_scale).astype(jnp.bfloat16)
    key_term = jnp.einsum('cqk,cqd->ckd', wide_score_grad.reshape(WIN, BLOCK, window_rows), wide_queries.reshape(WIN, BLOCK, HEAD_DIM)) * score_scale
    key_grad = lax.optimization_barrier(jnp.sum(lax.optimization_barrier(key_term.astype(jnp.bfloat16)).astype(jnp.float32), axis=0)).astype(jnp.bfloat16)
    value_term = jnp.einsum('cqk,cqd->ckd', rounded.astype(jnp.float32).reshape(WIN, BLOCK, window_rows), wide_grads.reshape(WIN, BLOCK, HEAD_DIM))
    value_grad = lax.optimization_barrier(jnp.sum(lax.optimization_barrier(value_term.astype(jnp.bfloat16)).astype(jnp.float32), axis=0)).astype(jnp.bfloat16)
    return (attended, query_grad, key_grad, value_grad)

def window_pass(stacked, doc_id, diag_kind):
    part_queries, part_keys, part_values, part_grads, part_slots = stacked
    window_rows = WIN * BLOCK
    token_index = jnp.arange(window_rows)
    row_in_stretch = token_index % BLOCK
    stretch_of = part_slots[token_index // BLOCK]
    doc_of = doc_id[stretch_of]
    full_of = diag_kind[stretch_of] == 0
    same_doc = doc_of[:, None] == doc_of[None, :]
    earlier = stretch_of[None, :] < stretch_of[:, None]
    same_stretch = stretch_of[None, :] == stretch_of[:, None]
    lower_tri = row_in_stretch[None, :] <= row_in_stretch[:, None]
    allowed = same_doc & (earlier | same_stretch & (full_of[:, None] | lower_tri))

    def by_heads(array):
        return jnp.transpose(array.reshape(window_rows, HEADS, HEAD_DIM), (1, 0, 2))

    def by_rows(array):
        return jnp.transpose(array, (1, 0, 2)).reshape(window_rows, HEADS * HEAD_DIM)

    def per_head(head_stack):
        return head_pass(head_stack, allowed)
    attended, query_grad, key_grad, value_grad = lax.map(per_head, (by_heads(part_queries), by_heads(part_keys), by_heads(part_values), by_heads(part_grads)))
    return (by_rows(attended), by_rows(query_grad), by_rows(key_grad), by_rows(value_grad))

def reference(queries, key_rows, value_rows, out_grad, slot_stretch, doc_id, diag_kind):
    windows = STRETCHES // WIN
    window_rows = WIN * BLOCK
    features = HEADS * HEAD_DIM

    def per_window(stacked):
        return window_pass(stacked, doc_id, diag_kind)
    attended, query_grad, key_grad, value_grad = lax.map(per_window, (queries.reshape(windows, window_rows, features), key_rows.reshape(windows, window_rows, features), value_rows.reshape(windows, window_rows, features), out_grad.reshape(windows, window_rows, features), slot_stretch.reshape(windows, WIN)))
    return (attended.reshape(TOKENS, features), query_grad.reshape(TOKENS, features), key_grad.reshape(TOKENS, features), value_grad.reshape(TOKENS, features))
```

```python
import functools
import math

import jax
import jax.numpy as jnp
from jax import lax
from jax.experimental import pallas as pl
from jax.experimental.pallas import tpu as pltpu
from jax.sharding import PartitionSpec as P

HEAD_DIM = 128
BLOCK = 128
WIN = 16
GROUP = 8
HEADS_HERE = 6
HP = 4
PIECE = 64
PIECES = WIN * BLOCK // PIECE
ARRAYS = 4
MESH = pl.DeviceIdType.MESH
SCALE = 1.0 / math.sqrt(HEAD_DIM)
CHUNK = 256


def owner_of(head):
    return head + jnp.where(head >= 1, 1, 0) + jnp.where(head >= 5, 1, 0)


def head_of(member):
    return member - jnp.where(member >= 2, 1, 0) - jnp.where(member >= 7, 1, 0)


def is_owner(member):
    return (member != 1) & (member != 6)


def spread_kernel(*refs):
    sources, (landed, send_sem, recv_sem) = refs[:ARRAYS], refs[ARRAYS:]
    cp, hp = lax.axis_index("cp"), lax.axis_index("hp")
    member = lax.rem(cp, GROUP)
    first = cp - member
    owner = is_owner(member)

    barrier = pltpu.get_barrier_semaphore()

    @pl.when(owner)
    def _():
        for other in range(1, GROUP):
            peer = first + lax.rem(member + other, GROUP)
            pl.semaphore_signal(barrier, inc=1, device_id=(peer, hp), device_id_type=MESH)

    pl.semaphore_wait(barrier, HEADS_HERE - jnp.where(owner, 1, 0))

    rows = pl.ds(pl.multiple_of(member * 2 * BLOCK, 2 * BLOCK), 2 * BLOCK)

    def remote(array, step):
        head = jnp.where(member < GROUP // 2, HEADS_HERE - 1 - step, step)
        target = owner_of(head)
        columns = pl.ds(pl.multiple_of(head * HEAD_DIM, HEAD_DIM), HEAD_DIM)
        return target, pltpu.make_async_remote_copy(
            src_ref=sources[array].at[:, columns],
            dst_ref=landed.at[array, rows],
            send_sem=send_sem.at[array, step],
            recv_sem=recv_sem.at[array, member],
            device_id=(first + target, hp),
            device_id_type=MESH,
        )

    def local(array):
        columns = pl.ds(pl.multiple_of(head_of(member) * HEAD_DIM, HEAD_DIM), HEAD_DIM)
        return pltpu.make_async_copy(
            sources[array].at[:, columns], landed.at[array, rows], recv_sem.at[array, member]
        )

    for array in range(ARRAYS):
        for step in range(HEADS_HERE):
            target, copy = remote(array, step)

            @pl.when(target != member)
            def _(copy=copy):
                copy.start()

        @pl.when(owner)
        def _(array=array):
            local(array).start()

    for array in range(ARRAYS):
        for step in range(HEADS_HERE):
            target, copy = remote(array, step)

            @pl.when(target != member)
            def _(copy=copy):
                copy.wait_send()

    @pl.when(owner)
    def _():
        for array in range(ARRAYS):
            for source in range(GROUP):
                pltpu.make_async_copy(
                    landed.at[array, pl.ds(source * 2 * BLOCK, 2 * BLOCK)],
                    landed.at[array, pl.ds(source * 2 * BLOCK, 2 * BLOCK)],
                    recv_sem.at[array, source],
                ).wait()


def spread(arrays):
    return pl.pallas_call(
        spread_kernel,
        name="spread_heads",
        out_shape=jax.ShapeDtypeStruct((ARRAYS, WIN * BLOCK, HEAD_DIM), jnp.bfloat16),
        in_specs=[pl.BlockSpec(memory_space=pl.ANY)] * ARRAYS,
        out_specs=pl.BlockSpec(memory_space=pl.ANY),
        scratch_shapes=[
            pltpu.SemaphoreType.DMA((ARRAYS, HEADS_HERE)),
            pltpu.SemaphoreType.DMA((ARRAYS, GROUP)),
        ],
        compiler_params=pltpu.CompilerParams(collective_id=0, has_side_effects=True),
    )(*arrays)


def matmul(left, right, left_dim, right_dim):
    return lax.dot_general(
        left, right, (((left_dim,), (right_dim,)), ((), ())), preferred_element_type=jnp.float32
    )


def attend_tile(width, stretch, slot, low, kind, refs):
    given, out, keys, values, key_acc, value_acc, scores, grads = refs
    chunks = width // CHUNK
    query, out_grad = given[0, slot], given[3, slot]
    base = jnp.maximum(stretch + 1 - width // BLOCK, 0)
    row = lax.broadcasted_iota(jnp.int32, (BLOCK, 1), 0)
    top = jnp.where(kind == 0, BLOCK, row + 1) + (stretch - base) * BLOCK
    bottom = (low - base) * BLOCK
    column = lax.broadcasted_iota(jnp.int32, (BLOCK, CHUNK), 1)

    def block(ref, chunk):
        return ref[pl.ds(base + 2 * chunk, 2)].reshape(CHUNK, HEAD_DIM)

    largest = None
    for chunk in range(chunks):
        score = matmul(query, block(keys, chunk), 1, 1)
        place = column + chunk * CHUNK
        score = jnp.where((place >= bottom) & (place < top), score, -1e30)
        scores[:, pl.ds(chunk * CHUNK, CHUNK)] = score
        grads[:, pl.ds(chunk * CHUNK, CHUNK)] = matmul(out_grad, block(values, chunk), 1, 1)
        largest = score if largest is None else jnp.maximum(largest, score)
    largest = jnp.max(largest, axis=1, keepdims=True)

    total = None
    for chunk in range(chunks):
        weight = jnp.exp((scores[:, pl.ds(chunk * CHUNK, CHUNK)] - largest) * SCALE)
        scores[:, pl.ds(chunk * CHUNK, CHUNK)] = weight
        total = weight if total is None else total + weight
    inverse = 1.0 / jnp.sum(total, axis=1, keepdims=True)

    attended = None
    for chunk in range(chunks):
        weight = scores[:, pl.ds(chunk * CHUNK, CHUNK)] * inverse
        scores[:, pl.ds(chunk * CHUNK, CHUNK)] = weight
        rounded = weight.astype(jnp.bfloat16)
        part = matmul(rounded, block(values, chunk), 1, 0)
        attended = part if attended is None else attended + part
        term = matmul(out_grad, rounded, 0, 0)
        value_acc[base + 2 * chunk] += term[:, :BLOCK]
        value_acc[base + 2 * chunk + 1] += term[:, BLOCK:]
    attended = attended.astype(jnp.bfloat16)
    grad_dot = jnp.sum(
        out_grad.astype(jnp.float32) * attended.astype(jnp.float32), axis=1, keepdims=True
    )

    query_grad = None
    for chunk in range(chunks):
        here = pl.ds(chunk * CHUNK, CHUNK)
        score_grad = (scores[:, here] * (grads[:, here] - grad_dot)).astype(jnp.bfloat16)
        part = matmul(score_grad, block(keys, chunk), 1, 0)
        query_grad = part if query_grad is None else query_grad + part
        term = matmul(query, score_grad, 0, 0)
        key_acc[base + 2 * chunk] += term[:, :BLOCK]
        key_acc[base + 2 * chunk + 1] += term[:, BLOCK:]
    query_grad = (query_grad * SCALE).astype(jnp.bfloat16)

    pieces = BLOCK // PIECE
    out[pl.ds(slot * pieces, pieces), 0] = attended.reshape(pieces, PIECE, HEAD_DIM)
    out[pl.ds(slot * pieces, pieces), 1] = query_grad.reshape(pieces, PIECE, HEAD_DIM)


def attend_kernel(
    window_of,
    slot_stretch,
    doc_id,
    diag_kind,
    given,
    out,
    keys,
    values,
    key_acc,
    value_acc,
    scores,
    grads,
    slot_of,
):
    window = window_of()
    first = window * WIN

    for slot in range(WIN):
        stretch = slot_stretch[first + slot] - first
        slot_of[stretch] = slot
        keys[stretch] = given[1, slot]
        values[stretch] = given[2, slot]
    key_acc[...] = jnp.zeros_like(key_acc)
    value_acc[...] = jnp.zeros_like(value_acc)
    refs = (given, out, keys, values, key_acc, value_acc, scores, grads)

    def one(stretch, carry):
        slot = slot_of[stretch]
        low = doc_id[first + stretch] - first
        kind = diag_kind[first + stretch]
        count = stretch + 1 - low
        least = 0
        for width in (256, 512, 1024, 2048):
            most = width // BLOCK

            @pl.when((count > least) & (count <= most))
            def _(width=width):
                attend_tile(width, stretch, slot, low, kind, refs)

            least = most
        return carry

    lax.fori_loop(0, WIN, one, 0)

    pieces = BLOCK // PIECE

    def finish(stretch, carry):
        slot = slot_of[stretch]
        key_grad = (key_acc[stretch] * SCALE).T.astype(jnp.bfloat16)
        value_grad = value_acc[stretch].T.astype(jnp.bfloat16)
        out[pl.ds(slot * pieces, pieces), 2] = key_grad.reshape(pieces, PIECE, HEAD_DIM)
        out[pl.ds(slot * pieces, pieces), 3] = value_grad.reshape(pieces, PIECE, HEAD_DIM)
        return carry

    lax.fori_loop(0, WIN, finish, 0)


def attend(given, slot_stretch, doc_id, diag_kind, window_of):
    whole = pl.BlockSpec(memory_space=pltpu.VMEM)
    scalars = pl.BlockSpec(memory_space=pltpu.SMEM)
    return pl.pallas_call(
        functools.partial(attend_kernel, window_of),
        name="attend_head",
        out_shape=jax.ShapeDtypeStruct((PIECES, ARRAYS, PIECE, HEAD_DIM), jnp.bfloat16),
        in_specs=[scalars, scalars, scalars, whole],
        out_specs=whole,
        scratch_shapes=[
            pltpu.VMEM((WIN, BLOCK, HEAD_DIM), jnp.bfloat16),
            pltpu.VMEM((WIN, BLOCK, HEAD_DIM), jnp.bfloat16),
            pltpu.VMEM((WIN, HEAD_DIM, BLOCK), jnp.float32),
            pltpu.VMEM((WIN, HEAD_DIM, BLOCK), jnp.float32),
            pltpu.VMEM((BLOCK, WIN * BLOCK), jnp.float32),
            pltpu.VMEM((BLOCK, WIN * BLOCK), jnp.float32),
            pltpu.SMEM((WIN,), jnp.int32),
        ],
        compiler_params=pltpu.CompilerParams(vmem_limit_bytes=48 * 1024 * 1024),
    )(slot_stretch, doc_id, diag_kind, given)


def collect_kernel(made, landed, send_sem, recv_sem, own_sem):
    cp, hp = lax.axis_index("cp"), lax.axis_index("hp")
    member = lax.rem(cp, GROUP)
    first = cp - member
    owner = is_owner(member)
    head = hp * HEADS_HERE + head_of(member)
    me = member * HP + hp

    barrier = pltpu.get_barrier_semaphore()

    def greet(step, carry):
        peer = lax.rem(me + step, PIECES)
        peer_member, peer_hp = peer // HP, lax.rem(peer, HP)

        @pl.when(is_owner(peer_member))
        def _():
            pl.semaphore_signal(
                barrier, inc=1, device_id=(first + peer_member, peer_hp), device_id_type=MESH
            )

        return carry

    lax.fori_loop(1, PIECES, greet, 0)

    def copy_to(step):
        peer = lax.rem(me + PIECES // 2 + step, PIECES)
        peer_member, peer_hp = peer // HP, lax.rem(peer, HP)
        return peer, pltpu.make_async_remote_copy(
            src_ref=made.at[peer],
            dst_ref=landed.at[head],
            send_sem=send_sem.at[step],
            recv_sem=recv_sem.at[head],
            device_id=(first + peer_member, peer_hp),
            device_id_type=MESH,
        )

    @pl.when(owner)
    def _():
        pl.semaphore_wait(barrier, PIECES - 1)

        def send(step, carry):
            peer, copy = copy_to(step)

            @pl.when(peer != me)
            def _():
                copy.start()

            return carry

        lax.fori_loop(0, PIECES, send, 0)
        pltpu.make_async_copy(made.at[me], landed.at[head], own_sem).start()

        def sent(step, carry):
            peer, copy = copy_to(step)

            @pl.when(peer != me)
            def _():
                copy.wait_send()

            return carry

        lax.fori_loop(0, PIECES, sent, 0)
        pltpu.make_async_copy(made.at[me], landed.at[head], own_sem).wait()

    def arrived(index, carry):
        @pl.when((index != head) | jnp.logical_not(owner))
        def _():
            pltpu.make_async_copy(landed.at[index], landed.at[index], recv_sem.at[index]).wait()

        return carry

    lax.fori_loop(0, HP * HEADS_HERE, arrived, 0)


def collect(made):
    heads = HP * HEADS_HERE
    return pl.pallas_call(
        collect_kernel,
        name="collect_heads",
        out_shape=jax.ShapeDtypeStruct((heads, ARRAYS, PIECE, HEAD_DIM), jnp.bfloat16),
        in_specs=[pl.BlockSpec(memory_space=pl.ANY)],
        out_specs=pl.BlockSpec(memory_space=pl.ANY),
        scratch_shapes=[
            pltpu.SemaphoreType.DMA((PIECES,)),
            pltpu.SemaphoreType.DMA((heads,)),
            pltpu.SemaphoreType.DMA,
        ],
        compiler_params=pltpu.CompilerParams(collective_id=1, has_side_effects=True),
    )(made)


def rows_kernel(landed, *outs):
    for array, out in enumerate(outs):
        for head in range(HP * HEADS_HERE):
            out[:, head * HEAD_DIM : (head + 1) * HEAD_DIM] = landed[head, array]


def rows(landed):
    whole = pl.BlockSpec(memory_space=pltpu.VMEM)
    shape = jax.ShapeDtypeStruct((PIECE, HP * HEADS_HERE * HEAD_DIM), jnp.bfloat16)
    return pl.pallas_call(
        rows_kernel,
        name="heads_to_rows",
        out_shape=[shape] * ARRAYS,
        in_specs=[whole],
        out_specs=[whole] * ARRAYS,
        compiler_params=pltpu.CompilerParams(vmem_limit_bytes=32 * 1024 * 1024),
    )(landed)


def body(queries, key_rows, value_rows, out_grad, slot_stretch, doc_id, diag_kind):
    landed = spread((queries, key_rows, value_rows, out_grad))
    made = attend(
        landed.reshape(ARRAYS, WIN, BLOCK, HEAD_DIM),
        slot_stretch,
        doc_id,
        diag_kind,
        lambda: lax.axis_index("cp") // GROUP,
    )
    return tuple(rows(collect(made)))


def solution(mesh):
    in_specs = (P("cp", "hp"), P("cp", "hp"), P("cp", "hp"), P("cp", "hp"), P(), P(), P())
    out_specs = (P(("cp", "hp"), None),) * 4
    return jax.shard_map(body, mesh=mesh, in_specs=in_specs, out_specs=out_specs, check_vma=False)
```

```python
import math

import jax
import jax.numpy as jnp
from jax import lax
from jax.experimental import pallas as pl
from jax.experimental.pallas import tpu as pltpu
from jax.sharding import PartitionSpec as P

HEAD_DIM = 128
BLOCK = 128
WIN = 16
ROWS = WIN * BLOCK
GROUP = 8
OWN_SLOTS = WIN // GROUP
HEADS_HERE = 6
HP = 4
PIECES = GROUP * HP
PIECE = ROWS // PIECES
ARRAYS = 4
CHUNK = 256
STEP = 4
MESH = pl.DeviceIdType.MESH
SCALE = 1.0 / math.sqrt(HEAD_DIM)


def owner_of(head):
    return head + jnp.where(head >= 1, 1, 0) + jnp.where(head >= 5, 1, 0)


def head_of(member):
    return member - jnp.where(member >= 2, 1, 0) - jnp.where(member >= 7, 1, 0)


def is_owner(member):
    return (member != 1) & (member != 6)


def matmul(left, right, left_dim, right_dim):
    return lax.dot_general(
        left, right, (((left_dim,), (right_dim,)), ((), ())), preferred_element_type=jnp.float32
    )


def block_rows(index):
    return pl.ds(pl.multiple_of(index * BLOCK, BLOCK), BLOCK)


def in_order(given, slot_of, ordered, turned):
    for stretch in range(WIN):
        here = pl.ds(stretch * BLOCK, BLOCK)
        block = given[slot_of[stretch]]
        ordered[here] = block
        if turned is not None:
            turned[:, here] = block.T


def to_slots(ordered, stretch_of, staged, array):
    for slot in range(WIN):
        staged[array, pl.ds(slot * BLOCK, BLOCK)] = ordered[stretch_of[slot]]


def by_rows(one):
    for band in range(WIN // STEP):

        def step(stretch, carry, band=band):
            one(stretch, (band + 1) * STEP * BLOCK)
            return carry

        lax.fori_loop(band * STEP, (band + 1) * STEP, step, 0)


def kernel(
    slot_stretch,
    doc_id,
    diag_kind,
    queries,
    key_rows,
    value_rows,
    out_grad,
    attended_out,
    query_out,
    key_out,
    value_out,
    given_queries,
    given_keys,
    given_values,
    given_grads,
    staged,
    query,
    key,
    value,
    grad,
    query_turned,
    grad_turned,
    attended,
    result,
    weights,
    score_grads,
    scores,
    give_sem,
    given_sem,
    send_sem,
    out_sem,
):
    sources = (queries, key_rows, value_rows, out_grad)
    given = (given_queries, given_keys, given_values, given_grads)
    outs = (attended_out, query_out, key_out, value_out)
    cp, hp = lax.axis_index("cp"), lax.axis_index("hp")
    member = lax.rem(cp, GROUP)
    first = cp - member
    owner = is_owner(member)
    own_head = head_of(member)
    me = member * HP + hp

    barrier = pltpu.get_barrier_semaphore()

    def greet(step, carry):
        peer = lax.rem(me + step, PIECES)
        peer_member, peer_hp = peer // HP, lax.rem(peer, HP)

        @pl.when(is_owner(peer_member) | (owner & (peer_hp == hp)))
        def _():
            pl.semaphore_signal(
                barrier, inc=1, device_id=(first + peer_member, peer_hp), device_id_type=MESH
            )

        return carry

    lax.fori_loop(1, PIECES, greet, 0)
    pl.semaphore_wait(barrier, jnp.where(owner, PIECES - 1, HEADS_HERE))

    own_slots = pl.ds(member * OWN_SLOTS, OWN_SLOTS)

    def give(array, step):
        head = jnp.where(member < GROUP // 2, HEADS_HERE - 1 - step, step)
        target = owner_of(head)
        columns = pl.ds(pl.multiple_of(head * HEAD_DIM, HEAD_DIM), HEAD_DIM)
        return target, pltpu.make_async_remote_copy(
            src_ref=sources[array].at[:, :, columns],
            dst_ref=given[array].at[own_slots],
            send_sem=give_sem.at[array, step],
            recv_sem=given_sem.at[array],
            device_id=(first + target, hp),
            device_id_type=MESH,
        )

    for array in range(ARRAYS):
        for step in range(HEADS_HERE):
            target, copy = give(array, step)

            @pl.when(target != member)
            def _(copy=copy):
                copy.start()

        @pl.when(owner)
        def _(array=array):
            columns = pl.ds(pl.multiple_of(own_head * HEAD_DIM, HEAD_DIM), HEAD_DIM)
            pltpu.make_async_copy(
                sources[array].at[:, :, columns], given[array].at[own_slots], given_sem.at[array]
            ).start()

    def arrived(array):
        pltpu.make_async_copy(given[array], given[array], given_sem.at[array]).wait()

    def out_columns():
        return pl.ds(
            pl.multiple_of((hp * HEADS_HERE + own_head) * HEAD_DIM, HEAD_DIM), HEAD_DIM
        )

    def piece_rows(piece):
        return pl.ds(pl.multiple_of(piece * PIECE, PIECE), PIECE)

    def send(array):
        def one(step, carry):
            peer = lax.rem(me + PIECES // 2 + step, PIECES)
            peer_member, peer_hp = peer // HP, lax.rem(peer, HP)

            @pl.when(peer != me)
            def _():
                pltpu.make_async_remote_copy(
                    src_ref=staged.at[array, piece_rows(peer)],
                    dst_ref=outs[array].at[:, out_columns()],
                    send_sem=send_sem.at[array],
                    recv_sem=out_sem.at[array],
                    device_id=(first + peer_member, peer_hp),
                    device_id_type=MESH,
                ).start()

            return carry

        lax.fori_loop(0, PIECES, one, 0)
        pltpu.make_async_copy(
            staged.at[array, piece_rows(me)], outs[array].at[:, out_columns()], out_sem.at[array]
        ).start()

    @pl.when(owner)
    def _():
        base = (first // GROUP) * WIN
        stretch_of = [lax.rem(slot_stretch[base + slot], WIN) for slot in range(WIN)]
        slot_of = []
        for stretch in range(WIN):
            place = jnp.int32(0)
            for slot in range(1, WIN):
                place = jnp.where(stretch_of[slot] == stretch, slot, place)
            slot_of.append(place)

        arrived(0)
        in_order(given[0], slot_of, query, query_turned)
        arrived(1)
        in_order(given[1], slot_of, key, None)

        row = lax.broadcasted_iota(jnp.int32, (BLOCK, 1), 0)
        column = lax.broadcasted_iota(jnp.int32, (BLOCK, CHUNK), 1)

        def weigh(stretch, width):
            here = block_rows(stretch)
            bottom = (doc_id[base + stretch] - base) * BLOCK
            top = jnp.where(diag_kind[base + stretch] == 0, BLOCK, row + 1) + stretch * BLOCK
            own = query[here]
            largest = None
            for start in range(0, width, CHUNK):
                score = matmul(own, key[pl.ds(start, CHUNK)], 1, 1)
                place = column + start
                score = jnp.where((place >= bottom) & (place < top), score, -1e30)
                scores[:, pl.ds(start, CHUNK)] = score
                largest = score if largest is None else jnp.maximum(largest, score)
            largest = jnp.max(largest, axis=1, keepdims=True)
            total = None
            for start in range(0, width, CHUNK):
                weight = jnp.exp((scores[:, pl.ds(start, CHUNK)] - largest) * SCALE)
                scores[:, pl.ds(start, CHUNK)] = weight
                total = weight if total is None else total + weight
            inverse = 1.0 / jnp.sum(total, axis=1, keepdims=True)
            for start in range(0, width, CHUNK):
                weight = scores[:, pl.ds(start, CHUNK)] * inverse
                weights[here, pl.ds(start, CHUNK)] = weight.astype(jnp.bfloat16)

        by_rows(weigh)

        arrived(2)
        in_order(given[2], slot_of, value, None)

        def forward(stretch, width):
            here = block_rows(stretch)
            attended[stretch] = matmul(
                weights[here, pl.ds(0, width)], value[pl.ds(0, width)], 1, 0
            ).astype(jnp.bfloat16)

        by_rows(forward)
        to_slots(attended, stretch_of, staged, 0)
        send(0)

        arrived(3)
        in_order(given[3], slot_of, grad, grad_turned)

        def over_queries(turned, pairs, factor):
            for start in range(0, ROWS, CHUNK):
                rest = pl.ds(start, ROWS - start)
                here = pl.ds(start, CHUNK)
                term = matmul(turned[:, rest], pairs[rest, here], 1, 0)
                if factor is not None:
                    term = term * factor
                turned_back = term.T.astype(jnp.bfloat16)
                result[start // BLOCK] = turned_back[:BLOCK]
                result[start // BLOCK + 1] = turned_back[BLOCK:]

        over_queries(grad_turned, weights, None)
        to_slots(result, stretch_of, staged, 3)
        send(3)

        def backward(stretch, width):
            here = block_rows(stretch)
            own = grad[here]
            grad_dot = jnp.sum(
                own.astype(jnp.float32) * attended[stretch].astype(jnp.float32), axis=1, keepdims=True
            )
            for start in range(0, width, CHUNK):
                columns = pl.ds(start, CHUNK)
                weight_grad = matmul(own, value[columns], 1, 1)
                weight = weights[here, columns].astype(jnp.float32)
                score_grads[here, columns] = (weight * (weight_grad - grad_dot)).astype(
                    jnp.bfloat16
                )
            query_grad = matmul(score_grads[here, pl.ds(0, width)], key[pl.ds(0, width)], 1, 0)
            result[stretch] = (query_grad * SCALE).astype(jnp.bfloat16)

        by_rows(backward)
        to_slots(result, stretch_of, staged, 1)
        send(1)

        over_queries(query_turned, score_grads, SCALE)
        to_slots(result, stretch_of, staged, 2)
        send(2)

    for array in range(ARRAYS):
        for step in range(HEADS_HERE):
            target, copy = give(array, step)

            @pl.when(target != member)
            def _(copy=copy):
                copy.wait_send()

    @pl.when(owner)
    def _():
        for array in range(ARRAYS):
            gone = staged.at[array, pl.ds(0, ROWS - PIECE)]
            pltpu.make_async_copy(gone, gone, send_sem.at[array]).wait()

    for array in range(ARRAYS):
        pltpu.make_async_copy(outs[array], outs[array], out_sem.at[array]).wait()


def body(queries, key_rows, value_rows, out_grad, slot_stretch, doc_id, diag_kind):
    anywhere = pl.BlockSpec(memory_space=pl.ANY)
    scalars = pl.BlockSpec(memory_space=pltpu.SMEM)
    shape = jax.ShapeDtypeStruct((PIECE, HP * HEADS_HERE * HEAD_DIM), jnp.bfloat16)
    ordered = pltpu.VMEM((ROWS, HEAD_DIM), jnp.bfloat16)
    stacked = pltpu.VMEM((WIN, BLOCK, HEAD_DIM), jnp.bfloat16)
    turned = pltpu.VMEM((HEAD_DIM, ROWS), jnp.bfloat16)
    pairs = pltpu.VMEM((ROWS, ROWS), jnp.bfloat16)
    arrays = [
        array.reshape(OWN_SLOTS, BLOCK, HEADS_HERE * HEAD_DIM)
        for array in (queries, key_rows, value_rows, out_grad)
    ]
    return tuple(
        pl.pallas_call(
            kernel,
            name="attend_windows",
            out_shape=[shape] * ARRAYS,
            in_specs=[scalars] * 3 + [anywhere] * ARRAYS,
            out_specs=[anywhere] * ARRAYS,
            scratch_shapes=[
                stacked,
                stacked,
                stacked,
                stacked,
                pltpu.VMEM((ARRAYS, ROWS, HEAD_DIM), jnp.bfloat16),
                ordered,
                ordered,
                ordered,
                ordered,
                turned,
                turned,
                stacked,
                stacked,
                pairs,
                pairs,
                pltpu.VMEM((BLOCK, ROWS), jnp.float32),
                pltpu.SemaphoreType.DMA((ARRAYS, HEADS_HERE)),
                pltpu.SemaphoreType.DMA((ARRAYS,)),
                pltpu.SemaphoreType.DMA((ARRAYS,)),
                pltpu.SemaphoreType.DMA((ARRAYS,)),
            ],
            compiler_params=pltpu.CompilerParams(
                collective_id=0, has_side_effects=True, vmem_limit_bytes=48 * 1024 * 1024
            ),
        )(slot_stretch, doc_id, diag_kind, *arrays)
    )


def solution(mesh):
    in_specs = (P("cp", "hp"), P("cp", "hp"), P("cp", "hp"), P("cp", "hp"), P(), P(), P())
    out_specs = (P(("cp", "hp"), None),) * 4
    return jax.shard_map(body, mesh=mesh, in_specs=in_specs, out_specs=out_specs, check_vma=False)
```

```python
import math

import jax
import jax.numpy as jnp
from jax import lax
from jax.experimental import pallas as pl
from jax.experimental.pallas import tpu as pltpu
from jax.sharding import PartitionSpec as P

HEAD_DIM = 128
BLOCK = 128
WIN = 16
ROWS = WIN * BLOCK
GROUP = 8
OWN_SLOTS = WIN // GROUP
HEADS_HERE = 6
HP = 4
PIECES = GROUP * HP
PIECE = ROWS // PIECES
ARRAYS = 4
CHUNK = 256
STEP = 4
MESH = pl.DeviceIdType.MESH
SCALE = 1.0 / math.sqrt(HEAD_DIM)


def owner_of(head):
    return head + jnp.where(head >= 1, 1, 0) + jnp.where(head >= 5, 1, 0)


def head_of(member):
    return member - jnp.where(member >= 2, 1, 0) - jnp.where(member >= 7, 1, 0)


def is_owner(member):
    return (member != 1) & (member != 6)


def matmul(left, right, left_dim, right_dim):
    return lax.dot_general(
        left, right, (((left_dim,), (right_dim,)), ((), ())), preferred_element_type=jnp.float32
    )


def block_rows(index):
    return pl.ds(pl.multiple_of(index * BLOCK, BLOCK), BLOCK)


def in_order(given, slot_of, ordered, turned):
    for stretch in range(WIN):
        here = pl.ds(stretch * BLOCK, BLOCK)
        block = given[slot_of[stretch]]
        ordered[here] = block
        if turned is not None:
            turned[:, here] = block.T


def to_slots(ordered, stretch_of, staged, array):
    for slot in range(WIN):
        staged[array, pl.ds(slot * BLOCK, BLOCK)] = ordered[stretch_of[slot]]


def by_rows(one):
    for band in range(WIN // STEP):

        def step(stretch, carry, band=band):
            one(stretch, (band + 1) * STEP * BLOCK)
            return carry

        lax.fori_loop(band * STEP, (band + 1) * STEP, step, 0)


def kernel(
    slot_stretch,
    doc_id,
    diag_kind,
    queries,
    key_rows,
    value_rows,
    out_grad,
    attended_out,
    query_out,
    key_out,
    value_out,
    given_queries,
    given_keys,
    given_values,
    given_grads,
    staged,
    query,
    key,
    value,
    grad,
    query_turned,
    grad_turned,
    attended,
    result,
    weights,
    score_grads,
    scores,
    give_sem,
    given_sem,
    send_sem,
    out_sem,
):
    sources = (queries, key_rows, value_rows, out_grad)
    given = (given_queries, given_keys, given_values, given_grads)
    outs = (attended_out, query_out, key_out, value_out)
    cp, hp = lax.axis_index("cp"), lax.axis_index("hp")
    member = lax.rem(cp, GROUP)
    first = cp - member
    owner = is_owner(member)
    own_head = head_of(member)
    me = member * HP + hp

    barrier = pltpu.get_barrier_semaphore()

    def greet(step, carry):
        peer = lax.rem(me + step, PIECES)
        peer_member, peer_hp = peer // HP, lax.rem(peer, HP)

        @pl.when(is_owner(peer_member) | (owner & (peer_hp == hp)))
        def _():
            pl.semaphore_signal(
                barrier, inc=1, device_id=(first + peer_member, peer_hp), device_id_type=MESH
            )

        return carry

    lax.fori_loop(1, PIECES, greet, 0)
    pl.semaphore_wait(barrier, jnp.where(owner, PIECES - 1, HEADS_HERE))

    own_slots = pl.ds(member * OWN_SLOTS, OWN_SLOTS)

    def give(array, step):
        head = jnp.where(member < GROUP // 2, HEADS_HERE - 1 - step, step)
        target = owner_of(head)
        columns = pl.ds(pl.multiple_of(head * HEAD_DIM, HEAD_DIM), HEAD_DIM)
        return target, pltpu.make_async_remote_copy(
            src_ref=sources[array].at[:, :, columns],
            dst_ref=given[array].at[own_slots],
            send_sem=give_sem.at[array, step],
            recv_sem=given_sem.at[array],
            device_id=(first + target, hp),
            device_id_type=MESH,
        )

    for array in range(ARRAYS):
        for step in range(HEADS_HERE):
            target, copy = give(array, step)

            @pl.when(target != member)
            def _(copy=copy):
                copy.start()

        @pl.when(owner)
        def _(array=array):
            columns = pl.ds(pl.multiple_of(own_head * HEAD_DIM, HEAD_DIM), HEAD_DIM)
            pltpu.make_async_copy(
                sources[array].at[:, :, columns], given[array].at[own_slots], given_sem.at[array]
            ).start()

    def arrived(array):
        pltpu.make_async_copy(given[array], given[array], given_sem.at[array]).wait()

    def out_columns():
        return pl.ds(
            pl.multiple_of((hp * HEADS_HERE + own_head) * HEAD_DIM, HEAD_DIM), HEAD_DIM
        )

    def piece_rows(piece):
        return pl.ds(pl.multiple_of(piece * PIECE, PIECE), PIECE)

    def send(array):
        def one(step, carry):
            peer = lax.rem(me + PIECES // 2 + step, PIECES)
            peer_member, peer_hp = peer // HP, lax.rem(peer, HP)

            @pl.when(peer != me)
            def _():
                pltpu.make_async_remote_copy(
                    src_ref=staged.at[array, piece_rows(peer)],
                    dst_ref=outs[array].at[:, out_columns()],
                    send_sem=send_sem.at[array],
                    recv_sem=out_sem.at[array],
                    device_id=(first + peer_member, peer_hp),
                    device_id_type=MESH,
                ).start()

            return carry

        lax.fori_loop(0, PIECES, one, 0)
        pltpu.make_async_copy(
            staged.at[array, piece_rows(me)], outs[array].at[:, out_columns()], out_sem.at[array]
        ).start()

    @pl.when(owner)
    def _():
        base = (first // GROUP) * WIN
        stretch_of = [lax.rem(slot_stretch[base + slot], WIN) for slot in range(WIN)]
        slot_of = []
        for stretch in range(WIN):
            place = jnp.int32(0)
            for slot in range(1, WIN):
                place = jnp.where(stretch_of[slot] == stretch, slot, place)
            slot_of.append(place)

        arrived(0)
        in_order(given[0], slot_of, query, query_turned)
        arrived(1)
        in_order(given[1], slot_of, key, None)

        row = lax.broadcasted_iota(jnp.int32, (BLOCK, 1), 0)
        column = lax.broadcasted_iota(jnp.int32, (BLOCK, CHUNK), 1)

        def weigh(stretch, width):
            here = block_rows(stretch)
            bottom = (doc_id[base + stretch] - base) * BLOCK
            top = jnp.where(diag_kind[base + stretch] == 0, BLOCK, row + 1) + stretch * BLOCK
            own = query[here]
            largest = None
            for start in range(0, width, CHUNK):
                score = matmul(own, key[pl.ds(start, CHUNK)], 1, 1)
                place = column + start
                score = jnp.where((place >= bottom) & (place < top), score, -1e30)
                scores[:, pl.ds(start, CHUNK)] = score
                largest = score if largest is None else jnp.maximum(largest, score)
            largest = jnp.max(largest, axis=1, keepdims=True)
            total = None
            for start in range(0, width, CHUNK):
                weight = jnp.exp((scores[:, pl.ds(start, CHUNK)] - largest) * SCALE)
                scores[:, pl.ds(start, CHUNK)] = weight
                total = weight if total is None else total + weight
            inverse = 1.0 / jnp.sum(total, axis=1, keepdims=True)
            for start in range(0, width, CHUNK):
                weight = scores[:, pl.ds(start, CHUNK)] * inverse
                weights[here, pl.ds(start, CHUNK)] = weight.astype(jnp.bfloat16)

        by_rows(weigh)

        arrived(2)
        in_order(given[2], slot_of, value, None)

        def forward(stretch, width):
            here = block_rows(stretch)
            attended[stretch] = matmul(
                weights[here, pl.ds(0, width)], value[pl.ds(0, width)], 1, 0
            ).astype(jnp.bfloat16)

        by_rows(forward)
        to_slots(attended, stretch_of, staged, 0)
        send(0)

        arrived(3)
        in_order(given[3], slot_of, grad, grad_turned)

        def over_queries(turned, pairs, factor):
            for start in range(0, ROWS, CHUNK):
                rest = pl.ds(start, ROWS - start)
                here = pl.ds(start, CHUNK)
                term = matmul(turned[:, rest], pairs[rest, here], 1, 0)
                if factor is not None:
                    term = term * factor
                turned_back = term.T.astype(jnp.bfloat16)
                result[start // BLOCK] = turned_back[:BLOCK]
                result[start // BLOCK + 1] = turned_back[BLOCK:]

        over_queries(grad_turned, weights, None)
        to_slots(result, stretch_of, staged, 3)
        send(3)

        def backward(stretch, width):
            here = block_rows(stretch)
            own = grad[here]
            grad_dot = jnp.sum(
                own.astype(jnp.float32) * attended[stretch].astype(jnp.float32), axis=1, keepdims=True
            )
            for start in range(0, width, CHUNK):
                columns = pl.ds(start, CHUNK)
                weight_grad = matmul(own, value[columns], 1, 1)
                weight = weights[here, columns].astype(jnp.float32)
                score_grads[here, columns] = (weight * (weight_grad - grad_dot)).astype(
                    jnp.bfloat16
                )
            query_grad = matmul(score_grads[here, pl.ds(0, width)], key[pl.ds(0, width)], 1, 0)
            result[stretch] = (query_grad * SCALE).astype(jnp.bfloat16)

        by_rows(backward)
        to_slots(result, stretch_of, staged, 1)
        send(1)

        over_queries(query_turned, score_grads, SCALE)
        to_slots(result, stretch_of, staged, 2)
        send(2)

    for array in range(ARRAYS):
        for step in range(HEADS_HERE):
            target, copy = give(array, step)

            @pl.when(target != member)
            def _(copy=copy):
                copy.wait_send()

    @pl.when(owner)
    def _():
        for array in range(ARRAYS):
            gone = staged.at[array, pl.ds(0, ROWS - PIECE)]
            pltpu.make_async_copy(gone, gone, send_sem.at[array]).wait()

    for array in range(ARRAYS):
        pltpu.make_async_copy(outs[array], outs[array], out_sem.at[array]).wait()


def settle_kernel(*refs):
    landed, outs = refs[:ARRAYS], refs[ARRAYS : 2 * ARRAYS]
    held, in_sems, out_sems = refs[2 * ARRAYS :]
    coming = [
        pltpu.make_async_copy(landed[array], held.at[array], in_sems.at[array])
        for array in range(ARRAYS)
    ]
    going = [
        pltpu.make_async_copy(held.at[array], outs[array], out_sems.at[array])
        for array in range(ARRAYS)
    ]
    for copy in coming:
        copy.start()
    for array in range(ARRAYS):
        coming[array].wait()
        going[array].start()
    for copy in going:
        copy.wait()


def settle(landed):
    anywhere = pl.BlockSpec(memory_space=pl.ANY)
    return pl.pallas_call(
        settle_kernel,
        name="settle_results",
        out_shape=[jax.ShapeDtypeStruct(array.shape, array.dtype) for array in landed],
        in_specs=[anywhere] * ARRAYS,
        out_specs=[anywhere] * ARRAYS,
        scratch_shapes=[
            pltpu.VMEM((ARRAYS, *landed[0].shape), jnp.bfloat16),
            pltpu.SemaphoreType.DMA((ARRAYS,)),
            pltpu.SemaphoreType.DMA((ARRAYS,)),
        ],
    )(*landed)


def body(queries, key_rows, value_rows, out_grad, slot_stretch, doc_id, diag_kind):
    anywhere = pl.BlockSpec(memory_space=pl.ANY)
    scalars = pl.BlockSpec(memory_space=pltpu.SMEM)
    shape = jax.ShapeDtypeStruct((PIECE, HP * HEADS_HERE * HEAD_DIM), jnp.bfloat16)
    ordered = pltpu.VMEM((ROWS, HEAD_DIM), jnp.bfloat16)
    stacked = pltpu.VMEM((WIN, BLOCK, HEAD_DIM), jnp.bfloat16)
    turned = pltpu.VMEM((HEAD_DIM, ROWS), jnp.bfloat16)
    pairs = pltpu.VMEM((ROWS, ROWS), jnp.bfloat16)
    arrays = [
        array.reshape(OWN_SLOTS, BLOCK, HEADS_HERE * HEAD_DIM)
        for array in (queries, key_rows, value_rows, out_grad)
    ]
    landed = (
        pl.pallas_call(
            kernel,
            name="attend_windows",
            out_shape=[shape] * ARRAYS,
            in_specs=[scalars] * 3 + [anywhere] * ARRAYS,
            out_specs=[anywhere] * ARRAYS,
            scratch_shapes=[
                stacked,
                stacked,
                stacked,
                stacked,
                pltpu.VMEM((ARRAYS, ROWS, HEAD_DIM), jnp.bfloat16),
                ordered,
                ordered,
                ordered,
                ordered,
                turned,
                turned,
                stacked,
                stacked,
                pairs,
                pairs,
                pltpu.VMEM((BLOCK, ROWS), jnp.float32),
                pltpu.SemaphoreType.DMA((ARRAYS, HEADS_HERE)),
                pltpu.SemaphoreType.DMA((ARRAYS,)),
                pltpu.SemaphoreType.DMA((ARRAYS,)),
                pltpu.SemaphoreType.DMA((ARRAYS,)),
            ],
            compiler_params=pltpu.CompilerParams(
                collective_id=0, has_side_effects=True, vmem_limit_bytes=62 * 1024 * 1024
            ),
        )(slot_stretch, doc_id, diag_kind, *arrays)
    )
    return tuple(settle(landed))


def solution(mesh):
    in_specs = (P("cp", "hp"), P("cp", "hp"), P("cp", "hp"), P("cp", "hp"), P(), P(), P())
    out_specs = (P(("cp", "hp"), None),) * 4
    return jax.shard_map(body, mesh=mesh, in_specs=in_specs, out_specs=out_specs, check_vma=False)
```

```python
import math

import jax
import jax.numpy as jnp
from jax import lax
from jax.experimental import pallas as pl
from jax.experimental.pallas import tpu as pltpu
from jax.sharding import PartitionSpec as P

HEAD_DIM = 128
BLOCK = 128
WIN = 16
ROWS = WIN * BLOCK
GROUP = 8
OWN_SLOTS = WIN // GROUP
HEADS_HERE = 6
HP = 4
PIECES = GROUP * HP
PIECE = ROWS // PIECES
ARRAYS = 4
CHUNK = 256
STEP = 4
MESH = pl.DeviceIdType.MESH
SCALE = 1.0 / math.sqrt(HEAD_DIM)


def owner_of(head):
    return head + jnp.where(head >= 1, 1, 0) + jnp.where(head >= 5, 1, 0)


def head_of(member):
    return member - jnp.where(member >= 2, 1, 0) - jnp.where(member >= 7, 1, 0)


def is_owner(member):
    return (member != 1) & (member != 6)


def matmul(left, right, left_dim, right_dim):
    return lax.dot_general(
        left, right, (((left_dim,), (right_dim,)), ((), ())), preferred_element_type=jnp.float32
    )


def block_rows(index):
    return pl.ds(pl.multiple_of(index * BLOCK, BLOCK), BLOCK)


def in_order(given, slot_of, ordered, turned):
    for stretch in range(WIN):
        here = pl.ds(stretch * BLOCK, BLOCK)
        block = given[slot_of[stretch]]
        ordered[here] = block
        if turned is not None:
            turned[:, here] = block.T


def to_slots(ordered, stretch_of, staged, array):
    for slot in range(WIN):
        staged[array, pl.ds(slot * BLOCK, BLOCK)] = ordered[stretch_of[slot]]


def by_rows(one):
    for band in range(WIN // STEP):

        def step(stretch, carry, band=band):
            one(stretch, (band + 1) * STEP * BLOCK)
            return carry

        lax.fori_loop(band * STEP, (band + 1) * STEP, step, 0)


def kernel(
    slot_stretch,
    doc_id,
    diag_kind,
    queries,
    key_rows,
    value_rows,
    out_grad,
    attended_out,
    query_out,
    key_out,
    value_out,
    given_queries,
    given_keys,
    given_values,
    given_grads,
    staged,
    query,
    key,
    value,
    grad,
    query_turned,
    grad_turned,
    attended,
    result,
    weights,
    score_grads,
    scores,
    give_sem,
    given_sem,
    send_sem,
    out_sem,
    ready,
):
    sources = (queries, key_rows, value_rows, out_grad)
    given = (given_queries, given_keys, given_values, given_grads)
    outs = (attended_out, query_out, key_out, value_out)
    cp, hp = lax.axis_index("cp"), lax.axis_index("hp")
    member = lax.rem(cp, GROUP)
    first = cp - member
    owner = is_owner(member)
    own_head = head_of(member)
    me = member * HP + hp

    barrier = pltpu.get_barrier_semaphore()

    for step in range(1, GROUP):
        peer = lax.rem(member + step, GROUP)

        @pl.when(owner | is_owner(peer))
        def _(peer=peer):
            pl.semaphore_signal(
                barrier, inc=1, device_id=(first + peer, hp), device_id_type=MESH
            )

    def greet_beside(semaphore):
        for step in range(1, HP):
            pl.semaphore_signal(
                semaphore, inc=1, device_id=(cp, lax.rem(hp + step, HP)), device_id_type=MESH
            )

    @pl.when(owner)
    def _():
        greet_beside(barrier)

    pl.semaphore_wait(barrier, jnp.where(owner, GROUP - 1 + HP - 1, HEADS_HERE))

    own_slots = pl.ds(member * OWN_SLOTS, OWN_SLOTS)

    def give(array, step):
        head = jnp.where(member < GROUP // 2, HEADS_HERE - 1 - step, step)
        target = owner_of(head)
        columns = pl.ds(pl.multiple_of(head * HEAD_DIM, HEAD_DIM), HEAD_DIM)
        return target, pltpu.make_async_remote_copy(
            src_ref=sources[array].at[:, :, columns],
            dst_ref=given[array].at[own_slots],
            send_sem=give_sem.at[array, step],
            recv_sem=given_sem.at[array],
            device_id=(first + target, hp),
            device_id_type=MESH,
        )

    for array in range(ARRAYS):
        for step in range(HEADS_HERE):
            target, copy = give(array, step)

            @pl.when(target != member)
            def _(copy=copy):
                copy.start()

        @pl.when(owner)
        def _(array=array):
            columns = pl.ds(pl.multiple_of(own_head * HEAD_DIM, HEAD_DIM), HEAD_DIM)
            pltpu.make_async_copy(
                sources[array].at[:, :, columns], given[array].at[own_slots], given_sem.at[array]
            ).start()

    @pl.when(owner)
    def _():
        greet_beside(ready)

    def arrived(array):
        pltpu.make_async_copy(given[array], given[array], given_sem.at[array]).wait()

    def out_columns():
        return pl.ds(
            pl.multiple_of((hp * HEADS_HERE + own_head) * HEAD_DIM, HEAD_DIM), HEAD_DIM
        )

    def piece_rows(piece):
        return pl.ds(pl.multiple_of(piece * PIECE, PIECE), PIECE)

    def send(array):
        def one(step, carry):
            peer_member = member ^ (GROUP // 2 ^ step // HP)
            peer_hp = lax.rem(step, HP)
            peer = peer_member * HP + peer_hp

            @pl.when(peer != me)
            def _():
                pltpu.make_async_remote_copy(
                    src_ref=staged.at[array, piece_rows(peer)],
                    dst_ref=outs[array].at[:, out_columns()],
                    send_sem=send_sem.at[array],
                    recv_sem=out_sem.at[array],
                    device_id=(first + peer_member, peer_hp),
                    device_id_type=MESH,
                ).start()

            return carry

        lax.fori_loop(0, PIECES, one, 0)
        pltpu.make_async_copy(
            staged.at[array, piece_rows(me)], outs[array].at[:, out_columns()], out_sem.at[array]
        ).start()

    @pl.when(owner)
    def _():
        base = (first // GROUP) * WIN
        stretch_of = [lax.rem(slot_stretch[base + slot], WIN) for slot in range(WIN)]
        slot_of = []
        for stretch in range(WIN):
            place = jnp.int32(0)
            for slot in range(1, WIN):
                place = jnp.where(stretch_of[slot] == stretch, slot, place)
            slot_of.append(place)

        arrived(0)
        in_order(given[0], slot_of, query, query_turned)
        arrived(1)
        in_order(given[1], slot_of, key, None)

        row = lax.broadcasted_iota(jnp.int32, (BLOCK, 1), 0)
        column = lax.broadcasted_iota(jnp.int32, (BLOCK, CHUNK), 1)

        def weigh(stretch, width):
            here = block_rows(stretch)
            bottom = (doc_id[base + stretch] - base) * BLOCK
            top = jnp.where(diag_kind[base + stretch] == 0, BLOCK, row + 1) + stretch * BLOCK
            own = query[here]
            largest = None
            for start in range(0, width, CHUNK):
                score = matmul(own, key[pl.ds(start, CHUNK)], 1, 1)
                place = column + start
                score = jnp.where((place >= bottom) & (place < top), score, -1e30)
                scores[:, pl.ds(start, CHUNK)] = score
                largest = score if largest is None else jnp.maximum(largest, score)
            largest = jnp.max(largest, axis=1, keepdims=True)
            total = None
            for start in range(0, width, CHUNK):
                weight = jnp.exp((scores[:, pl.ds(start, CHUNK)] - largest) * SCALE)
                scores[:, pl.ds(start, CHUNK)] = weight
                total = weight if total is None else total + weight
            inverse = 1.0 / jnp.sum(total, axis=1, keepdims=True)
            for start in range(0, width, CHUNK):
                weight = scores[:, pl.ds(start, CHUNK)] * inverse
                weights[here, pl.ds(start, CHUNK)] = weight.astype(jnp.bfloat16)

        by_rows(weigh)

        arrived(2)
        in_order(given[2], slot_of, value, None)

        def forward(stretch, width):
            here = block_rows(stretch)
            attended[stretch] = matmul(
                weights[here, pl.ds(0, width)], value[pl.ds(0, width)], 1, 0
            ).astype(jnp.bfloat16)

        by_rows(forward)
        to_slots(attended, stretch_of, staged, 0)
        pl.semaphore_wait(ready, HP - 1)
        send(0)

        arrived(3)
        in_order(given[3], slot_of, grad, grad_turned)

        def over_queries(turned, pairs, factor):
            for start in range(0, ROWS, CHUNK):
                rest = pl.ds(start, ROWS - start)
                here = pl.ds(start, CHUNK)
                term = matmul(turned[:, rest], pairs[rest, here], 1, 0)
                if factor is not None:
                    term = term * factor
                turned_back = term.T.astype(jnp.bfloat16)
                result[start // BLOCK] = turned_back[:BLOCK]
                result[start // BLOCK + 1] = turned_back[BLOCK:]

        over_queries(grad_turned, weights, None)
        to_slots(result, stretch_of, staged, 3)
        send(3)

        def backward(stretch, width):
            here = block_rows(stretch)
            own = grad[here]
            grad_dot = jnp.sum(
                own.astype(jnp.float32) * attended[stretch].astype(jnp.float32), axis=1, keepdims=True
            )
            for start in range(0, width, CHUNK):
                columns = pl.ds(start, CHUNK)
                weight_grad = matmul(own, value[columns], 1, 1)
                weight = weights[here, columns].astype(jnp.float32)
                score_grads[here, columns] = (weight * (weight_grad - grad_dot)).astype(
                    jnp.bfloat16
                )
            query_grad = matmul(score_grads[here, pl.ds(0, width)], key[pl.ds(0, width)], 1, 0)
            result[stretch] = (query_grad * SCALE).astype(jnp.bfloat16)

        by_rows(backward)
        to_slots(result, stretch_of, staged, 1)
        send(1)

        over_queries(query_turned, score_grads, SCALE)
        to_slots(result, stretch_of, staged, 2)
        send(2)

    for array in range(ARRAYS):
        for step in range(HEADS_HERE):
            target, copy = give(array, step)

            @pl.when(target != member)
            def _(copy=copy):
                copy.wait_send()

    @pl.when(owner)
    def _():
        for array in range(ARRAYS):
            gone = staged.at[array, pl.ds(0, ROWS - PIECE)]
            pltpu.make_async_copy(gone, gone, send_sem.at[array]).wait()

    for array in range(ARRAYS):
        pltpu.make_async_copy(outs[array], outs[array], out_sem.at[array]).wait()


def settle_kernel(*refs):
    landed, outs = refs[:ARRAYS], refs[ARRAYS : 2 * ARRAYS]
    held, in_sems, out_sems = refs[2 * ARRAYS :]
    coming = [
        pltpu.make_async_copy(landed[array], held.at[array], in_sems.at[array])
        for array in range(ARRAYS)
    ]
    going = [
        pltpu.make_async_copy(held.at[array], outs[array], out_sems.at[array])
        for array in range(ARRAYS)
    ]
    for copy in coming:
        copy.start()
    for array in range(ARRAYS):
        coming[array].wait()
        going[array].start()
    for copy in going:
        copy.wait()


def settle(landed):
    anywhere = pl.BlockSpec(memory_space=pl.ANY)
    return pl.pallas_call(
        settle_kernel,
        name="settle_results",
        out_shape=[jax.ShapeDtypeStruct(array.shape, array.dtype) for array in landed],
        in_specs=[anywhere] * ARRAYS,
        out_specs=[anywhere] * ARRAYS,
        scratch_shapes=[
            pltpu.VMEM((ARRAYS, *landed[0].shape), jnp.bfloat16),
            pltpu.SemaphoreType.DMA((ARRAYS,)),
            pltpu.SemaphoreType.DMA((ARRAYS,)),
        ],
    )(*landed)


def body(queries, key_rows, value_rows, out_grad, slot_stretch, doc_id, diag_kind):
    anywhere = pl.BlockSpec(memory_space=pl.ANY)
    scalars = pl.BlockSpec(memory_space=pltpu.SMEM)
    shape = jax.ShapeDtypeStruct((PIECE, HP * HEADS_HERE * HEAD_DIM), jnp.bfloat16)
    ordered = pltpu.VMEM((ROWS, HEAD_DIM), jnp.bfloat16)
    stacked = pltpu.VMEM((WIN, BLOCK, HEAD_DIM), jnp.bfloat16)
    turned = pltpu.VMEM((HEAD_DIM, ROWS), jnp.bfloat16)
    pairs = pltpu.VMEM((ROWS, ROWS), jnp.bfloat16)
    arrays = [
        array.reshape(OWN_SLOTS, BLOCK, HEADS_HERE * HEAD_DIM)
        for array in (queries, key_rows, value_rows, out_grad)
    ]
    landed = (
        pl.pallas_call(
            kernel,
            name="attend_windows",
            out_shape=[shape] * ARRAYS,
            in_specs=[scalars] * 3 + [anywhere] * ARRAYS,
            out_specs=[anywhere] * ARRAYS,
            scratch_shapes=[
                stacked,
                stacked,
                stacked,
                stacked,
                pltpu.VMEM((ARRAYS, ROWS, HEAD_DIM), jnp.bfloat16),
                ordered,
                ordered,
                ordered,
                ordered,
                turned,
                turned,
                stacked,
                stacked,
                pairs,
                pairs,
                pltpu.VMEM((BLOCK, ROWS), jnp.float32),
                pltpu.SemaphoreType.DMA((ARRAYS, HEADS_HERE)),
                pltpu.SemaphoreType.DMA((ARRAYS,)),
                pltpu.SemaphoreType.DMA((ARRAYS,)),
                pltpu.SemaphoreType.DMA((ARRAYS,)),
                pltpu.SemaphoreType.REGULAR,
            ],
            compiler_params=pltpu.CompilerParams(
                collective_id=0, has_side_effects=True, vmem_limit_bytes=62 * 1024 * 1024
            ),
        )(slot_stretch, doc_id, diag_kind, *arrays)
    )
    return tuple(settle(landed))


def solution(mesh):
    in_specs = (P("cp", "hp"), P("cp", "hp"), P("cp", "hp"), P("cp", "hp"), P(), P(), P())
    out_specs = (P(("cp", "hp"), None),) * 4
    return jax.shard_map(body, mesh=mesh, in_specs=in_specs, out_specs=out_specs, check_vma=False)
```

```python
import math

import jax
import jax.numpy as jnp
from jax import lax
from jax.experimental import pallas as pl
from jax.experimental.pallas import tpu as pltpu
from jax.sharding import PartitionSpec as P

HEAD_DIM = 128
BLOCK = 128
WIN = 16
ROWS = WIN * BLOCK
GROUP = 8
OWN_SLOTS = WIN // GROUP
HEADS_HERE = 6
HP = 4
PIECES = GROUP * HP
PIECE = ROWS // PIECES
ARRAYS = 4
CHUNK = 256
STEP = 4
MESH = pl.DeviceIdType.MESH
SCALE = 1.0 / math.sqrt(HEAD_DIM)


def owner_of(head):
    return head + jnp.where(head >= 1, 1, 0) + jnp.where(head >= 5, 1, 0)


def head_of(member):
    return member - jnp.where(member >= 2, 1, 0) - jnp.where(member >= 7, 1, 0)


def is_owner(member):
    return (member != 1) & (member != 6)


def rank_of(member):
    return lax.rem(member + GROUP - 1, GROUP)


def matmul(left, right, left_dim, right_dim):
    return lax.dot_general(
        left, right, (((left_dim,), (right_dim,)), ((), ())), preferred_element_type=jnp.float32
    )


def block_rows(index):
    return pl.ds(pl.multiple_of(index * BLOCK, BLOCK), BLOCK)


def in_order(given, slot_of, ordered, turned):
    for stretch in range(WIN):
        here = pl.ds(stretch * BLOCK, BLOCK)
        block = given[slot_of[stretch]]
        ordered[here] = block
        if turned is not None:
            turned[:, here] = block.T


def to_slots(ordered, stretch_of, staged, array):
    for slot in range(WIN):
        staged[array, pl.ds(slot * BLOCK, BLOCK)] = ordered[stretch_of[slot]]


def by_rows(one):
    for band in range(WIN // STEP):

        def step(stretch, carry, band=band):
            one(stretch, (band + 1) * STEP * BLOCK)
            return carry

        lax.fori_loop(band * STEP, (band + 1) * STEP, step, 0)


def kernel(
    slot_stretch_whole,
    doc_id_whole,
    diag_kind_whole,
    queries,
    key_rows,
    value_rows,
    out_grad,
    attended_out,
    query_out,
    key_out,
    value_out,
    slot_stretch,
    doc_id,
    diag_kind,
    given_queries,
    given_keys,
    given_values,
    given_grads,
    staged,
    query,
    key,
    value,
    grad,
    query_turned,
    grad_turned,
    attended,
    result,
    weights,
    score_grads,
    scores,
    give_sem,
    given_sem,
    send_sem,
    out_sem,
    ready,
    ready_beside,
    all_beside,
    table_sem,
):
    sources = (queries, key_rows, value_rows, out_grad)
    given = (given_queries, given_keys, given_values, given_grads)
    outs = (attended_out, query_out, key_out, value_out)
    cp, hp = lax.axis_index("cp"), lax.axis_index("hp")
    member = lax.rem(cp, GROUP)
    first = cp - member
    owner = is_owner(member)
    own_head = head_of(member)
    me = member * HP + hp

    tables = [
        pltpu.make_async_copy(whole, table, table_sem.at[index])
        for index, (whole, table) in enumerate(
            (
                (slot_stretch_whole, slot_stretch),
                (doc_id_whole, doc_id),
                (diag_kind_whole, diag_kind),
            )
        )
    ]

    barrier = pltpu.get_barrier_semaphore()

    def beside(semaphore, step):
        pl.semaphore_signal(
            semaphore, inc=1, device_id=(cp, lax.rem(hp + step, HP)), device_id_type=MESH
        )

    rank = rank_of(member)

    for step in range(1, GROUP):
        peer = lax.rem(member + step, GROUP)

        @pl.when((rank_of(peer) > rank) & (owner | is_owner(peer)))
        def _(peer=peer):
            pl.semaphore_signal(barrier, inc=1, device_id=(first + peer, hp), device_id_type=MESH)

    for step in range(1, HP):

        @pl.when(owner & (hp + step >= HP))
        def _(step=step):
            beside(barrier, step)

    lower_owners = rank - jnp.where(rank > 0, 1, 0)
    greetings = jnp.where(owner, rank + HP - 1 - hp, lower_owners)

    @pl.when(greetings > 0)
    def _():
        pl.semaphore_wait(barrier, greetings)

    for step in range(1, GROUP):
        peer = lax.rem(member + step, GROUP)

        @pl.when((rank_of(peer) < rank) & (owner | is_owner(peer)))
        def _(peer=peer):
            pl.semaphore_signal(
                ready.at[member], inc=1, device_id=(first + peer, hp), device_id_type=MESH
            )

    for step in range(1, HP):

        @pl.when(owner & (hp + step < HP))
        def _(step=step):
            beside(ready_beside, step)

    own_slots = pl.ds(member * OWN_SLOTS, OWN_SLOTS)

    def give(array, step):
        half = HEADS_HERE // 2
        if step < half:
            head = jnp.where(member < GROUP // 2, half + step, half - 1 - step)
        else:
            head = jnp.where(member < GROUP // 2, HEADS_HERE - 1 - step, step)
        target = owner_of(head)
        columns = pl.ds(pl.multiple_of(head * HEAD_DIM, HEAD_DIM), HEAD_DIM)
        return target, pltpu.make_async_remote_copy(
            src_ref=sources[array].at[:, :, columns],
            dst_ref=given[array].at[own_slots],
            send_sem=give_sem.at[array, step],
            recv_sem=given_sem.at[array],
            device_id=(first + target, hp),
            device_id_type=MESH,
        )

    for array in range(ARRAYS):
        for step in range(HEADS_HERE):
            target, copy = give(array, step)

            if array == 0:

                @pl.when(rank_of(target) > rank)
                def _(target=target):
                    pl.semaphore_wait(ready.at[target], 1)

            @pl.when(target != member)
            def _(copy=copy):
                copy.start()

        @pl.when(owner)
        def _(array=array):
            columns = pl.ds(pl.multiple_of(own_head * HEAD_DIM, HEAD_DIM), HEAD_DIM)
            pltpu.make_async_copy(
                sources[array].at[:, :, columns], given[array].at[own_slots], given_sem.at[array]
            ).start()

    @pl.when(owner)
    def _():
        for idle in (1, GROUP - 2):

            @pl.when(rank < idle - 1)
            def _(idle=idle):
                pl.semaphore_wait(ready.at[idle], 1)

        @pl.when(hp > 0)
        def _():
            pl.semaphore_wait(ready_beside, hp)

        for step in range(1, HP):
            beside(all_beside, step)

    for table in tables:
        table.start()
    for table in tables:
        table.wait()

    def arrived(array):
        pltpu.make_async_copy(given[array], given[array], given_sem.at[array]).wait()

    def out_columns():
        return pl.ds(
            pl.multiple_of((hp * HEADS_HERE + own_head) * HEAD_DIM, HEAD_DIM), HEAD_DIM
        )

    def piece_rows(piece):
        return pl.ds(pl.multiple_of(piece * PIECE, PIECE), PIECE)

    def send(array):
        def one(step, carry):
            peer_member = member ^ (GROUP // 2 ^ step // HP)
            peer_hp = lax.rem(step, HP)
            peer = peer_member * HP + peer_hp

            @pl.when(peer != me)
            def _():
                pltpu.make_async_remote_copy(
                    src_ref=staged.at[array, piece_rows(peer)],
                    dst_ref=outs[array].at[:, out_columns()],
                    send_sem=send_sem.at[array],
                    recv_sem=out_sem.at[array],
                    device_id=(first + peer_member, peer_hp),
                    device_id_type=MESH,
                ).start()

            return carry

        lax.fori_loop(0, PIECES, one, 0)
        pltpu.make_async_copy(
            staged.at[array, piece_rows(me)], outs[array].at[:, out_columns()], out_sem.at[array]
        ).start()

    @pl.when(owner)
    def _():
        base = (first // GROUP) * WIN
        stretch_of = [lax.rem(slot_stretch[base + slot], WIN) for slot in range(WIN)]
        slot_of = []
        for stretch in range(WIN):
            place = jnp.int32(0)
            for slot in range(1, WIN):
                place = jnp.where(stretch_of[slot] == stretch, slot, place)
            slot_of.append(place)

        arrived(0)
        in_order(given[0], slot_of, query, query_turned)
        arrived(1)
        in_order(given[1], slot_of, key, None)

        row = lax.broadcasted_iota(jnp.int32, (BLOCK, 1), 0)
        column = lax.broadcasted_iota(jnp.int32, (BLOCK, CHUNK), 1)

        def weigh(stretch, width):
            here = block_rows(stretch)
            bottom = (doc_id[base + stretch] - base) * BLOCK
            top = jnp.where(diag_kind[base + stretch] == 0, BLOCK, row + 1) + stretch * BLOCK
            own = query[here]
            largest = None
            for start in range(0, width, CHUNK):
                score = matmul(own, key[pl.ds(start, CHUNK)], 1, 1)
                place = column + start
                score = jnp.where((place >= bottom) & (place < top), score, -1e30)
                scores[:, pl.ds(start, CHUNK)] = score
                largest = score if largest is None else jnp.maximum(largest, score)
            largest = jnp.max(largest, axis=1, keepdims=True)
            total = None
            for start in range(0, width, CHUNK):
                weight = jnp.exp((scores[:, pl.ds(start, CHUNK)] - largest) * SCALE)
                scores[:, pl.ds(start, CHUNK)] = weight
                total = weight if total is None else total + weight
            inverse = 1.0 / jnp.sum(total, axis=1, keepdims=True)
            for start in range(0, width, CHUNK):
                weight = scores[:, pl.ds(start, CHUNK)] * inverse
                weights[here, pl.ds(start, CHUNK)] = weight.astype(jnp.bfloat16)

        by_rows(weigh)

        arrived(2)
        in_order(given[2], slot_of, value, None)

        def forward(stretch, width):
            here = block_rows(stretch)
            attended[stretch] = matmul(
                weights[here, pl.ds(0, width)], value[pl.ds(0, width)], 1, 0
            ).astype(jnp.bfloat16)

        by_rows(forward)
        to_slots(attended, stretch_of, staged, 0)
        pl.semaphore_wait(all_beside, HP - 1)
        send(0)

        arrived(3)
        in_order(given[3], slot_of, grad, grad_turned)

        def over_queries(turned, pairs, factor):
            for start in range(0, ROWS, CHUNK):
                rest = pl.ds(start, ROWS - start)
                here = pl.ds(start, CHUNK)
                term = matmul(turned[:, rest], pairs[rest, here], 1, 0)
                if factor is not None:
                    term = term * factor
                turned_back = term.T.astype(jnp.bfloat16)
                result[start // BLOCK] = turned_back[:BLOCK]
                result[start // BLOCK + 1] = turned_back[BLOCK:]

        over_queries(grad_turned, weights, None)
        to_slots(result, stretch_of, staged, 3)
        send(3)

        def backward(stretch, width):
            here = block_rows(stretch)
            own = grad[here]
            grad_dot = jnp.sum(
                own.astype(jnp.float32) * attended[stretch].astype(jnp.float32), axis=1, keepdims=True
            )
            for start in range(0, width, CHUNK):
                columns = pl.ds(start, CHUNK)
                weight_grad = matmul(own, value[columns], 1, 1)
                weight = weights[here, columns].astype(jnp.float32)
                score_grads[here, columns] = (weight * (weight_grad - grad_dot)).astype(
                    jnp.bfloat16
                )
            query_grad = matmul(score_grads[here, pl.ds(0, width)], key[pl.ds(0, width)], 1, 0)
            result[stretch] = (query_grad * SCALE).astype(jnp.bfloat16)

        by_rows(backward)
        to_slots(result, stretch_of, staged, 1)
        send(1)

        over_queries(query_turned, score_grads, SCALE)
        to_slots(result, stretch_of, staged, 2)
        send(2)

    for array in range(ARRAYS):
        for step in range(HEADS_HERE):
            target, copy = give(array, step)

            @pl.when(target != member)
            def _(copy=copy):
                copy.wait_send()

    @pl.when(owner)
    def _():
        for array in range(ARRAYS):
            gone = staged.at[array, pl.ds(0, ROWS - PIECE)]
            pltpu.make_async_copy(gone, gone, send_sem.at[array]).wait()

    for array in range(ARRAYS):
        pltpu.make_async_copy(outs[array], outs[array], out_sem.at[array]).wait()


def settle_kernel(*refs):
    landed, outs = refs[:ARRAYS], refs[ARRAYS : 2 * ARRAYS]
    held, in_sems, out_sems = refs[2 * ARRAYS :]
    coming = [
        pltpu.make_async_copy(landed[array], held.at[array], in_sems.at[array])
        for array in range(ARRAYS)
    ]
    going = [
        pltpu.make_async_copy(held.at[array], outs[array], out_sems.at[array])
        for array in range(ARRAYS)
    ]
    for copy in coming:
        copy.start()
    for array in range(ARRAYS):
        coming[array].wait()
        going[array].start()
    for copy in going:
        copy.wait()


def settle(landed):
    anywhere = pl.BlockSpec(memory_space=pl.ANY)
    return pl.pallas_call(
        settle_kernel,
        name="settle_results",
        out_shape=[jax.ShapeDtypeStruct(array.shape, array.dtype) for array in landed],
        in_specs=[anywhere] * ARRAYS,
        out_specs=[anywhere] * ARRAYS,
        scratch_shapes=[
            pltpu.VMEM((ARRAYS, *landed[0].shape), jnp.bfloat16),
            pltpu.SemaphoreType.DMA((ARRAYS,)),
            pltpu.SemaphoreType.DMA((ARRAYS,)),
        ],
    )(*landed)


def body(queries, key_rows, value_rows, out_grad, slot_stretch, doc_id, diag_kind):
    anywhere = pl.BlockSpec(memory_space=pl.ANY)
    shape = jax.ShapeDtypeStruct((PIECE, HP * HEADS_HERE * HEAD_DIM), jnp.bfloat16)
    ordered = pltpu.VMEM((ROWS, HEAD_DIM), jnp.bfloat16)
    stacked = pltpu.VMEM((WIN, BLOCK, HEAD_DIM), jnp.bfloat16)
    turned = pltpu.VMEM((HEAD_DIM, ROWS), jnp.bfloat16)
    pairs = pltpu.VMEM((ROWS, ROWS), jnp.bfloat16)
    arrays = [
        array.reshape(OWN_SLOTS, BLOCK, HEADS_HERE * HEAD_DIM)
        for array in (queries, key_rows, value_rows, out_grad)
    ]
    landed = (
        pl.pallas_call(
            kernel,
            name="attend_windows",
            out_shape=[shape] * ARRAYS,
            in_specs=[anywhere] * (3 + ARRAYS),
            out_specs=[anywhere] * ARRAYS,
            scratch_shapes=[
                *[pltpu.SMEM(table.shape, table.dtype) for table in (slot_stretch, doc_id, diag_kind)],
                stacked,
                stacked,
                stacked,
                stacked,
                pltpu.VMEM((ARRAYS, ROWS, HEAD_DIM), jnp.bfloat16),
                ordered,
                ordered,
                ordered,
                ordered,
                turned,
                turned,
                stacked,
                stacked,
                pairs,
                pairs,
                pltpu.VMEM((BLOCK, ROWS), jnp.float32),
                pltpu.SemaphoreType.DMA((ARRAYS, HEADS_HERE)),
                pltpu.SemaphoreType.DMA((ARRAYS,)),
                pltpu.SemaphoreType.DMA((ARRAYS,)),
                pltpu.SemaphoreType.DMA((ARRAYS,)),
                pltpu.SemaphoreType.REGULAR((GROUP,)),
                pltpu.SemaphoreType.REGULAR,
                pltpu.SemaphoreType.REGULAR,
                pltpu.SemaphoreType.DMA((3,)),
            ],
            compiler_params=pltpu.CompilerParams(
                collective_id=0, has_side_effects=True, vmem_limit_bytes=62 * 1024 * 1024
            ),
        )(slot_stretch, doc_id, diag_kind, *arrays)
    )
    return tuple(settle(landed))


def solution(mesh):
    in_specs = (P("cp", "hp"), P("cp", "hp"), P("cp", "hp"), P("cp", "hp"), P(), P(), P())
    out_specs = (P(("cp", "hp"), None),) * 4
    return jax.shard_map(body, mesh=mesh, in_specs=in_specs, out_specs=out_specs, check_vma=False)
```

```python
import math

import jax
import jax.numpy as jnp
from jax import lax
from jax.experimental import pallas as pl
from jax.experimental.pallas import tpu as pltpu
from jax.sharding import PartitionSpec as P

HEAD_DIM = 128
BLOCK = 128
WIN = 16
ROWS = WIN * BLOCK
GROUP = 8
OWN_SLOTS = WIN // GROUP
HEADS_HERE = 6
HP = 4
PIECES = GROUP * HP
PIECE = ROWS // PIECES
ARRAYS = 4
CHUNK = 256
STEP = 4
MESH = pl.DeviceIdType.MESH
SCALE = 1.0 / math.sqrt(HEAD_DIM)


def owner_of(head):
    return head + jnp.where(head >= 1, 1, 0) + jnp.where(head >= 5, 1, 0)


def head_of(member):
    return member - jnp.where(member >= 2, 1, 0) - jnp.where(member >= 7, 1, 0)


def is_owner(member):
    return (member != 1) & (member != 6)


def rank_of(member):
    return lax.rem(member + GROUP - 1, GROUP)


def matmul(left, right, left_dim, right_dim):
    return lax.dot_general(
        left, right, (((left_dim,), (right_dim,)), ((), ())), preferred_element_type=jnp.float32
    )


def block_rows(index):
    return pl.ds(pl.multiple_of(index * BLOCK, BLOCK), BLOCK)


def in_order(given, slot_of, ordered, turned):
    for stretch in range(WIN):
        here = pl.ds(stretch * BLOCK, BLOCK)
        block = given[slot_of[stretch]]
        ordered[here] = block
        if turned is not None:
            turned[:, here] = block.T


def to_slots(ordered, stretch_of, staged, array):
    for slot in range(WIN):
        staged[array, pl.ds(slot * BLOCK, BLOCK)] = ordered[stretch_of[slot]]


def by_rows(one):
    for band in range(WIN // STEP):

        def step(stretch, carry, band=band):
            one(stretch, (band + 1) * STEP * BLOCK)
            return carry

        lax.fori_loop(band * STEP, (band + 1) * STEP, step, 0)


def kernel(
    slot_stretch_whole,
    doc_id_whole,
    diag_kind_whole,
    queries,
    key_rows,
    value_rows,
    out_grad,
    attended_out,
    query_out,
    key_out,
    value_out,
    slot_stretch,
    doc_id,
    diag_kind,
    given_queries,
    given_keys,
    given_values,
    given_grads,
    staged,
    query,
    key,
    value,
    grad,
    query_turned,
    grad_turned,
    attended,
    result,
    weights,
    score_grads,
    scores,
    give_sem,
    given_sem,
    send_sem,
    out_sem,
    ready,
    ready_beside,
    all_beside,
    table_sem,
):
    sources = (queries, key_rows, value_rows, out_grad)
    given = (given_queries, given_keys, given_values, given_grads)
    outs = (attended_out, query_out, key_out, value_out)
    cp, hp = lax.axis_index("cp"), lax.axis_index("hp")
    member = lax.rem(cp, GROUP)
    first = cp - member
    owner = is_owner(member)
    own_head = head_of(member)
    me = member * HP + hp

    tables = [
        pltpu.make_async_copy(whole, table, table_sem.at[index])
        for index, (whole, table) in enumerate(
            (
                (slot_stretch_whole, slot_stretch),
                (doc_id_whole, doc_id),
                (diag_kind_whole, diag_kind),
            )
        )
    ]

    barrier = pltpu.get_barrier_semaphore()

    def beside(semaphore, step):
        pl.semaphore_signal(
            semaphore, inc=1, device_id=(cp, lax.rem(hp + step, HP)), device_id_type=MESH
        )

    rank = rank_of(member)

    for step in range(1, GROUP):
        peer = lax.rem(member + step, GROUP)

        @pl.when((rank_of(peer) > rank) & (owner | is_owner(peer)))
        def _(peer=peer):
            pl.semaphore_signal(barrier, inc=1, device_id=(first + peer, hp), device_id_type=MESH)

    for step in range(1, HP):

        @pl.when(owner & (hp + step >= HP))
        def _(step=step):
            beside(barrier, step)

    lower_owners = rank - jnp.where(rank > 0, 1, 0)
    greetings = jnp.where(owner, rank + HP - 1 - hp, lower_owners)

    @pl.when(greetings > 0)
    def _():
        pl.semaphore_wait(barrier, greetings)

    for step in range(1, GROUP):
        peer = lax.rem(member + step, GROUP)

        @pl.when((rank_of(peer) < rank) & (owner | is_owner(peer)))
        def _(peer=peer):
            pl.semaphore_signal(
                ready.at[member], inc=1, device_id=(first + peer, hp), device_id_type=MESH
            )

    for step in range(1, HP):

        @pl.when(owner & (hp + step < HP))
        def _(step=step):
            beside(ready_beside, step)

    own_slots = pl.ds(member * OWN_SLOTS, OWN_SLOTS)

    def give(array, step):
        half = HEADS_HERE // 2
        if step < half:
            head = jnp.where(member < GROUP // 2, half + step, half - 1 - step)
        else:
            head = jnp.where(member < GROUP // 2, HEADS_HERE - 1 - step, step)
        target = owner_of(head)
        columns = pl.ds(pl.multiple_of(head * HEAD_DIM, HEAD_DIM), HEAD_DIM)
        return target, pltpu.make_async_remote_copy(
            src_ref=sources[array].at[:, :, columns],
            dst_ref=given[array].at[own_slots],
            send_sem=give_sem.at[array, step],
            recv_sem=given_sem.at[array],
            device_id=(first + target, hp),
            device_id_type=MESH,
        )

    for array in range(ARRAYS):
        for step in range(HEADS_HERE):
            target, copy = give(array, step)

            if array == 0:

                @pl.when(rank_of(target) > rank)
                def _(target=target):
                    pl.semaphore_wait(ready.at[target], 1)

            @pl.when(target != member)
            def _(copy=copy):
                copy.start()

        @pl.when(owner)
        def _(array=array):
            columns = pl.ds(pl.multiple_of(own_head * HEAD_DIM, HEAD_DIM), HEAD_DIM)
            pltpu.make_async_copy(
                sources[array].at[:, :, columns], given[array].at[own_slots], given_sem.at[array]
            ).start()

    @pl.when(owner)
    def _():
        for idle in (1, GROUP - 2):

            @pl.when(rank < idle - 1)
            def _(idle=idle):
                pl.semaphore_wait(ready.at[idle], 1)

        @pl.when(hp > 0)
        def _():
            pl.semaphore_wait(ready_beside, hp)

        for step in range(1, HP):
            beside(all_beside, step)

    for table in tables:
        table.start()
    for table in tables:
        table.wait()

    def arrived(array):
        pltpu.make_async_copy(given[array], given[array], given_sem.at[array]).wait()

    def out_columns():
        return pl.ds(
            pl.multiple_of((hp * HEADS_HERE + own_head) * HEAD_DIM, HEAD_DIM), HEAD_DIM
        )

    def piece_rows(piece):
        return pl.ds(pl.multiple_of(piece * PIECE, PIECE), PIECE)

    def send(array):
        def one(step, carry):
            turn = step // HP
            peer_member = member ^ (jnp.where(turn < GROUP // 2, 4, 6) ^ turn)
            peer_hp = lax.rem(step, HP)
            peer = peer_member * HP + peer_hp

            @pl.when(peer != me)
            def _():
                pltpu.make_async_remote_copy(
                    src_ref=staged.at[array, piece_rows(peer)],
                    dst_ref=outs[array].at[:, out_columns()],
                    send_sem=send_sem.at[array],
                    recv_sem=out_sem.at[array],
                    device_id=(first + peer_member, peer_hp),
                    device_id_type=MESH,
                ).start()

            return carry

        lax.fori_loop(0, PIECES, one, 0)
        pltpu.make_async_copy(
            staged.at[array, piece_rows(me)], outs[array].at[:, out_columns()], out_sem.at[array]
        ).start()

    @pl.when(owner)
    def _():
        base = (first // GROUP) * WIN
        stretch_of = [lax.rem(slot_stretch[base + slot], WIN) for slot in range(WIN)]
        slot_of = []
        for stretch in range(WIN):
            place = jnp.int32(0)
            for slot in range(1, WIN):
                place = jnp.where(stretch_of[slot] == stretch, slot, place)
            slot_of.append(place)

        arrived(0)
        in_order(given[0], slot_of, query, query_turned)
        arrived(1)
        in_order(given[1], slot_of, key, None)

        row = lax.broadcasted_iota(jnp.int32, (BLOCK, 1), 0)
        column = lax.broadcasted_iota(jnp.int32, (BLOCK, CHUNK), 1)

        def weigh(stretch, width):
            here = block_rows(stretch)
            bottom = (doc_id[base + stretch] - base) * BLOCK
            top = jnp.where(diag_kind[base + stretch] == 0, BLOCK, row + 1) + stretch * BLOCK
            own = query[here]
            largest = None
            for start in range(0, width, CHUNK):
                score = matmul(own, key[pl.ds(start, CHUNK)], 1, 1)
                place = column + start
                score = jnp.where((place >= bottom) & (place < top), score, -1e30)
                scores[:, pl.ds(start, CHUNK)] = score
                largest = score if largest is None else jnp.maximum(largest, score)
            largest = jnp.max(largest, axis=1, keepdims=True)
            total = None
            for start in range(0, width, CHUNK):
                weight = jnp.exp((scores[:, pl.ds(start, CHUNK)] - largest) * SCALE)
                scores[:, pl.ds(start, CHUNK)] = weight
                total = weight if total is None else total + weight
            inverse = 1.0 / jnp.sum(total, axis=1, keepdims=True)
            for start in range(0, width, CHUNK):
                weight = scores[:, pl.ds(start, CHUNK)] * inverse
                weights[here, pl.ds(start, CHUNK)] = weight.astype(jnp.bfloat16)

        by_rows(weigh)

        arrived(2)
        in_order(given[2], slot_of, value, None)

        def forward(stretch, width):
            here = block_rows(stretch)
            attended[stretch] = matmul(
                weights[here, pl.ds(0, width)], value[pl.ds(0, width)], 1, 0
            ).astype(jnp.bfloat16)

        by_rows(forward)
        to_slots(attended, stretch_of, staged, 0)
        pl.semaphore_wait(all_beside, HP - 1)
        send(0)

        arrived(3)
        in_order(given[3], slot_of, grad, grad_turned)

        def over_queries(turned, pairs, factor):
            for start in range(0, ROWS, CHUNK):
                rest = pl.ds(start, ROWS - start)
                here = pl.ds(start, CHUNK)
                term = matmul(turned[:, rest], pairs[rest, here], 1, 0)
                if factor is not None:
                    term = term * factor
                turned_back = term.T.astype(jnp.bfloat16)
                result[start // BLOCK] = turned_back[:BLOCK]
                result[start // BLOCK + 1] = turned_back[BLOCK:]

        over_queries(grad_turned, weights, None)
        to_slots(result, stretch_of, staged, 3)
        send(3)

        def backward(stretch, width):
            here = block_rows(stretch)
            own = grad[here]
            grad_dot = jnp.sum(
                own.astype(jnp.float32) * attended[stretch].astype(jnp.float32), axis=1, keepdims=True
            )
            for start in range(0, width, CHUNK):
                columns = pl.ds(start, CHUNK)
                weight_grad = matmul(own, value[columns], 1, 1)
                weight = weights[here, columns].astype(jnp.float32)
                score_grads[here, columns] = (weight * (weight_grad - grad_dot)).astype(
                    jnp.bfloat16
                )
            query_grad = matmul(score_grads[here, pl.ds(0, width)], key[pl.ds(0, width)], 1, 0)
            result[stretch] = (query_grad * SCALE).astype(jnp.bfloat16)

        by_rows(backward)
        to_slots(result, stretch_of, staged, 1)
        send(1)

        over_queries(query_turned, score_grads, SCALE)
        to_slots(result, stretch_of, staged, 2)
        send(2)

    for array in range(ARRAYS):
        for step in range(HEADS_HERE):
            target, copy = give(array, step)

            @pl.when(target != member)
            def _(copy=copy):
                copy.wait_send()

    @pl.when(owner)
    def _():
        for array in range(ARRAYS):
            gone = staged.at[array, pl.ds(0, ROWS - PIECE)]
            pltpu.make_async_copy(gone, gone, send_sem.at[array]).wait()

    for array in range(ARRAYS):
        pltpu.make_async_copy(outs[array], outs[array], out_sem.at[array]).wait()


def settle_kernel(*refs):
    landed, outs = refs[:ARRAYS], refs[ARRAYS : 2 * ARRAYS]
    held, in_sems, out_sems = refs[2 * ARRAYS :]
    coming = [
        pltpu.make_async_copy(landed[array], held.at[array], in_sems.at[array])
        for array in range(ARRAYS)
    ]
    going = [
        pltpu.make_async_copy(held.at[array], outs[array], out_sems.at[array])
        for array in range(ARRAYS)
    ]
    for copy in coming:
        copy.start()
    for array in range(ARRAYS):
        coming[array].wait()
        going[array].start()
    for copy in going:
        copy.wait()


def settle(landed):
    anywhere = pl.BlockSpec(memory_space=pl.ANY)
    return pl.pallas_call(
        settle_kernel,
        name="settle_results",
        out_shape=[jax.ShapeDtypeStruct(array.shape, array.dtype) for array in landed],
        in_specs=[anywhere] * ARRAYS,
        out_specs=[anywhere] * ARRAYS,
        scratch_shapes=[
            pltpu.VMEM((ARRAYS, *landed[0].shape), jnp.bfloat16),
            pltpu.SemaphoreType.DMA((ARRAYS,)),
            pltpu.SemaphoreType.DMA((ARRAYS,)),
        ],
    )(*landed)


def body(queries, key_rows, value_rows, out_grad, slot_stretch, doc_id, diag_kind):
    anywhere = pl.BlockSpec(memory_space=pl.ANY)
    shape = jax.ShapeDtypeStruct((PIECE, HP * HEADS_HERE * HEAD_DIM), jnp.bfloat16)
    ordered = pltpu.VMEM((ROWS, HEAD_DIM), jnp.bfloat16)
    stacked = pltpu.VMEM((WIN, BLOCK, HEAD_DIM), jnp.bfloat16)
    turned = pltpu.VMEM((HEAD_DIM, ROWS), jnp.bfloat16)
    pairs = pltpu.VMEM((ROWS, ROWS), jnp.bfloat16)
    arrays = [
        array.reshape(OWN_SLOTS, BLOCK, HEADS_HERE * HEAD_DIM)
        for array in (queries, key_rows, value_rows, out_grad)
    ]
    landed = (
        pl.pallas_call(
            kernel,
            name="attend_windows",
            out_shape=[shape] * ARRAYS,
            in_specs=[anywhere] * (3 + ARRAYS),
            out_specs=[anywhere] * ARRAYS,
            scratch_shapes=[
                *[pltpu.SMEM(table.shape, table.dtype) for table in (slot_stretch, doc_id, diag_kind)],
                stacked,
                stacked,
                stacked,
                stacked,
                pltpu.VMEM((ARRAYS, ROWS, HEAD_DIM), jnp.bfloat16),
                ordered,
                ordered,
                ordered,
                ordered,
                turned,
                turned,
                stacked,
                stacked,
                pairs,
                pairs,
                pltpu.VMEM((BLOCK, ROWS), jnp.float32),
                pltpu.SemaphoreType.DMA((ARRAYS, HEADS_HERE)),
                pltpu.SemaphoreType.DMA((ARRAYS,)),
                pltpu.SemaphoreType.DMA((ARRAYS,)),
                pltpu.SemaphoreType.DMA((ARRAYS,)),
                pltpu.SemaphoreType.REGULAR((GROUP,)),
                pltpu.SemaphoreType.REGULAR,
                pltpu.SemaphoreType.REGULAR,
                pltpu.SemaphoreType.DMA((3,)),
            ],
            compiler_params=pltpu.CompilerParams(
                collective_id=0, has_side_effects=True, vmem_limit_bytes=62 * 1024 * 1024
            ),
        )(slot_stretch, doc_id, diag_kind, *arrays)
    )
    return tuple(settle(landed))


def solution(mesh):
    in_specs = (P("cp", "hp"), P("cp", "hp"), P("cp", "hp"), P("cp", "hp"), P(), P(), P())
    out_specs = (P(("cp", "hp"), None),) * 4
    return jax.shard_map(body, mesh=mesh, in_specs=in_specs, out_specs=out_specs, check_vma=False)
```
